512 devices in a mesh: ctx: 16 (over x, y_hi, core), head: 32 (over z, y_lo).
Axes of the slice: x: 4, y: 4 (y_hi: 2, y_lo: 2; y = y_hi * 2 + y_lo), z: 16, core: 2. Of those that a mesh axis runs over, the one named last changes fastest.
Arguments:
- query: bfloat16 [65536, 4096], P(('ctx', 'head')), may hold values from -13 to 13
- key: bfloat16 [65536, 512], P(('ctx', 'head')), may hold values from -8 to 8
- value: bfloat16 [65536, 512], P(('ctx', 'head')), may hold values from -6 to 6
- attn_out: bfloat16 [65536, 4096], P(('ctx', 'head')), may hold values from -6 to 6
- out_grad: bfloat16 [65536, 4096], P(('ctx', 'head')), may hold values from -6 to 6
- segments: int32 [65536], P(('ctx', 'head')), may hold values from 0 to 255, never falling along the last dimension, each value on 1 to 512 neighbouring positions
Outputs:
- query_grad: bfloat16 [65536, 4096], P(('ctx', 'head'))
- key_grad: bfloat16 [65536, 512], P(('ctx', 'head'))
- value_grad: bfloat16 [65536, 512], P(('ctx', 'head'))
The draws below stay inside these ranges and needn't reach their ends.
Inputs may be any that keep to these rules, and one draw needn't show every extreme that they name: `segments`: never falls along positions; each document spans at most 512 positions, and one spans exactly 512.
All inputs are finite; a program needn't handle non-finite values.
Results may differ from the reference program's by a relative error of at most 0.0057.
Values may be sent and summed in bfloat16 or wider, within the bound.
No kernel may reach another device: no remote copies, remote signals or barrier semaphores. Data moves between devices by JAX's collectives and lax.ppermute only.
A program may use at most 64 MiB of HBM per device.

```python
import math
import jax
import jax.numpy as jnp
import numpy as np
from jax import lax

HEAD_DIM = 128
MOST = 512
HEADS = 32
KV_HEADS = 4
TOKENS = 65536
DOCS = 256


def draw_query(key, part):
    key = jax.random.fold_in(key, 11)
    first = jax.random.fold_in(key, 0)
    base = jnp.clip(jax.random.normal(first, (TOKENS, HEADS * HEAD_DIM), jnp.float32), -4.5, 4.5)
    return base.astype(jnp.bfloat16)


def draw_key(key, part):
    key = jax.random.fold_in(key, 23)
    base = jnp.clip(jax.random.normal(key, (TOKENS, KV_HEADS * HEAD_DIM), jnp.float32), -4.5, 4.5)
    return base.astype(jnp.bfloat16)


def shard_levels(key, shape, cuts, least, largest):
    gain = 1.0
    for axis_at, parts in cuts:
        heights = jax.random.uniform(jax.random.fold_in(jax.random.fold_in(key, 6), axis_at), (parts,), jnp.float32, least / len(cuts), largest / len(cuts))
        gain = gain * jnp.repeat(jnp.exp(heights), shape[axis_at] // parts).reshape((-1,) + (1,) * (len(shape) - 1 - axis_at))
    return gain


def length_profile(amount, total, limit, lean):
    weights = [(1 << 20) // math.isqrt(grade ** lean) + 1 for grade in range(2, amount + 1)]
    spare, counts = total - limit - (amount - 1), [1] * (amount - 1)
    while spare > 0:
        free = [i for i in range(amount - 1) if counts[i] < limit]
        pool, left = sum([weights[i] for i in free]), spare
        for i in free:
            extra = min(limit - counts[i], max(1, left * weights[i] // pool), spare)
            counts[i] = counts[i] + extra
            spare = spare - extra
    return np.array([limit] + counts)


def ragged(own_key, count, total, most, slope):
    if count == 2:
        one = jax.random.randint(own_key, (), max(1, total - most), min(most, total - 1) + 1)
        return jnp.stack([one, total - one])
    sizes = jnp.asarray(length_profile(count, total, most, slope), jnp.int32)
    pairs = (count - 1) // 2
    source_of, taker = sizes[1:1 + 2 * pairs:2], sizes[2:2 + 2 * pairs:2]
    room = jnp.minimum(source_of - 1, most - taker)
    passed = jax.random.randint(jax.random.fold_in(own_key, 1), (pairs,), 0, 1 << 20) % (room + 1)
    sizes = sizes.at[1:1 + 2 * pairs:2].set(source_of - passed).at[2:2 + 2 * pairs:2].set(taker + passed)
    return sizes[jax.random.permutation(jax.random.fold_in(own_key, 2), count)]


def gaussian(stream_key, extent, width, limit, shards=(), kind=jnp.bfloat16):
    gain = shard_levels(stream_key, extent, shards, -0.22, 0.18) if shards else 1.0
    values = jax.random.normal(stream_key, extent, jnp.float32) * width * gain
    return jnp.minimum(jnp.maximum(values, -limit), limit).astype(kind)


def setup_inputs(seed: int = 0) -> dict:
    key_of = jax.random.split(jax.random.key(seed), 7)
    query = draw_query(jax.random.fold_in(key_of[6], 71), 0)
    key = draw_key(jax.random.fold_in(key_of[6], 71), 0)
    value = gaussian(key_of[2], (TOKENS, KV_HEADS * HEAD_DIM), 1.0, 6.0, ((0, 512),))
    attn_out = gaussian(key_of[3], (TOKENS, HEADS * HEAD_DIM), 1.0, 6.0, ((0, 512),))
    out_grad = gaussian(key_of[4], (TOKENS, HEADS * HEAD_DIM), 1.0, 6.0, ((0, 512),))
    segments = jnp.searchsorted(jnp.cumsum(ragged(key_of[5], DOCS, TOKENS, MOST, 1)), jnp.arange(TOKENS), side="right").astype(jnp.int32)
    return dict(query=query, key=key, value=value, attn_out=attn_out, out_grad=out_grad, segments=segments)


def block_math(q_blk, k_blk, v_blk, g_blk, delta_blk, allowed, scale):
    s = jnp.einsum('qhd,khd->hqk', q_blk, k_blk) * scale
    s = jnp.where(allowed[None], s, -jnp.inf)
    top = jnp.max(s, axis=-1, keepdims=True)
    total = jnp.sum(jnp.exp(s - top), axis=-1, keepdims=True)
    prob = jnp.exp(s - (top + jnp.log(total)))
    dprob = jnp.einsum('qhd,khd->hqk', g_blk, v_blk)
    dscore = prob * (dprob - jnp.transpose(delta_blk)[:, :, None])
    prob_low = prob.astype(jnp.bfloat16).astype(jnp.float32)
    dscore_low = dscore.astype(jnp.bfloat16).astype(jnp.float32)
    dq = jnp.einsum('hqk,khd->qhd', dscore_low, k_blk) * scale
    dk = jnp.einsum('hqk,qhd->khd', dscore_low, q_blk) * scale
    dv = jnp.einsum('hqk,qhd->khd', prob_low, g_blk)
    return dq, dk, dv


def reference(query, key, value, attn_out, out_grad, segments):
    span = MOST
    heads = HEADS
    kv_heads = KV_HEADS
    group = heads // kv_heads
    total_rows = query.shape[0]
    scale = HEAD_DIM ** -0.5
    q3 = query.reshape(total_rows, heads, HEAD_DIM)
    g3 = out_grad.reshape(total_rows, heads, HEAD_DIM)
    delta = jnp.sum(g3.astype(jnp.float32) * attn_out.reshape(total_rows, heads, HEAD_DIM).astype(jnp.float32), axis=2)
    pad_kv = jnp.zeros((span, kv_heads, HEAD_DIM), jnp.bfloat16)
    k_pad = jnp.concatenate([pad_kv, key.reshape(total_rows, kv_heads, HEAD_DIM)], axis=0)
    v_pad = jnp.concatenate([pad_kv, value.reshape(total_rows, kv_heads, HEAD_DIM)], axis=0)
    seg_pad = jnp.concatenate([jnp.full((span,), -1, jnp.int32), segments.astype(jnp.int32)], axis=0)
    offsets = jnp.arange(span, dtype=jnp.int32)
    wide_offsets = jnp.arange(2 * span, dtype=jnp.int32)

    def finish(heads_grad):
        rounded = lax.optimization_barrier(heads_grad.astype(jnp.bfloat16))
        summed = rounded.astype(jnp.float32).reshape(span, kv_heads, group, HEAD_DIM).sum(axis=2)
        return summed.astype(jnp.bfloat16).reshape(span, kv_heads * HEAD_DIM)

    def step(carry, block):
        pend_k, pend_v = carry
        start = (block * span).astype(jnp.int32)
        q_blk = lax.dynamic_slice_in_dim(q3, start, span, 0).astype(jnp.float32)
        g_blk = lax.dynamic_slice_in_dim(g3, start, span, 0).astype(jnp.float32)
        d_blk = lax.dynamic_slice_in_dim(delta, start, span, 0)
        k_blk = jnp.repeat(lax.dynamic_slice_in_dim(k_pad, start, 2 * span, 0), group, axis=1).astype(jnp.float32)
        v_blk = jnp.repeat(lax.dynamic_slice_in_dim(v_pad, start, 2 * span, 0), group, axis=1).astype(jnp.float32)
        seg_q = lax.dynamic_slice_in_dim(segments.astype(jnp.int32), start, span, 0)
        seg_k = lax.dynamic_slice_in_dim(seg_pad, start, 2 * span, 0)
        q_pos = start + offsets
        k_pos = start - span + wide_offsets
        allowed = (seg_q[:, None] == seg_k[None, :]) & (k_pos[None, :] <= q_pos[:, None]) & (k_pos[None, :] >= 0)
        dq, dk, dv = block_math(q_blk, k_blk, v_blk, g_blk, d_blk, allowed, scale)
        out_k = finish(pend_k + dk[:span])
        out_v = finish(pend_v + dv[:span])
        dq_low = dq.astype(jnp.bfloat16).reshape(span, heads * HEAD_DIM)
        return (dk[span:], dv[span:]), (dq_low, out_k, out_v)

    init = (jnp.zeros((span, heads, HEAD_DIM), jnp.float32), jnp.zeros((span, heads, HEAD_DIM), jnp.float32))
    blocks = jnp.arange(total_rows // span, dtype=jnp.int32)
    (last_k, last_v), (dq_all, dk_all, dv_all) = lax.scan(step, init, blocks)
    query_grad = dq_all.reshape(total_rows, heads * HEAD_DIM)
    key_grad = jnp.concatenate([dk_all[1:].reshape(-1, kv_heads * HEAD_DIM), finish(last_k)], axis=0)
    value_grad = jnp.concatenate([dv_all[1:].reshape(-1, kv_heads * HEAD_DIM), finish(last_v)], axis=0)
    return query_grad, key_grad, value_grad
```

```python
import functools
import math

import jax
import jax.numpy as jnp
from jax import lax
from jax.experimental import pallas as pl
from jax.experimental.pallas import tpu as pltpu
from jax.sharding import PartitionSpec as P

HEAD_DIM = 128
MOST = 512
CHUNKS = 1
SCALE = HEAD_DIM ** (-0.5)
LOG2_SCALE = SCALE * math.log2(math.e)
HIDDEN = -1e30
AXES = ("ctx", "head")
NT = (((1,), (1,)), ((), ()))
NN = (((1,), (0,)), ((), ()))


def shift(value, steps):
    count = lax.axis_size(AXES)
    return lax.ppermute(value, AXES, [(i, i + steps) for i in range(count) if 0 <= i + steps < count])


def swap(value):
    return lax.ppermute(value, "head", [(i, i ^ 1) for i in range(lax.axis_size("head"))])


def dot(a, b, dims):
    return lax.dot_general(a, b, dims, preferred_element_type=jnp.float32)


def delta_kernel(g_ref, o_ref, delta_ref):
    for h in range(delta_ref.shape[0]):
        cols = slice(h * HEAD_DIM, (h + 1) * HEAD_DIM)
        prod = g_ref[:, cols].astype(jnp.float32) * o_ref[:, cols].astype(jnp.float32)
        delta_ref[h : h + 1, :] = jnp.sum(prod.T, axis=0, keepdims=True)


def row_delta(out_grad, attn_out):
    tok, width = out_grad.shape
    return pl.pallas_call(
        delta_kernel,
        out_shape=jax.ShapeDtypeStruct((width // HEAD_DIM, tok), jnp.float32),
        cost_estimate=pl.CostEstimate(flops=2 * tok * width, bytes_accessed=4 * tok * width, transcendentals=0),
        name="row_delta",
    )(out_grad, attn_out)


def attention_kernel(
    tok, group, kv_heads,
    q_ref, g_ref, delta_ref, own_ref, b1_ref, a1_ref, b2_ref, a2_ref,
    dq_ref, own_out, d1_out, d2_out, d3_out, d4_out,
    bias_scr, p_scr, ds_scr,
):
    pieces = (a2_ref, b2_ref, a1_ref, b1_ref, own_ref)
    outs = (d4_out, d3_out, d2_out, d1_out, own_out)

    def documents(ref):
        rows = ref[2 * tok : 2 * tok + 16, :tok].astype(jnp.float32)
        return jnp.concatenate([rows] * (tok // 16), axis=0)

    mine = documents(own_ref)
    for at, ref in enumerate(pieces):
        same = documents(ref).T == mine
        if ref is own_ref:
            key_at = lax.broadcasted_iota(jnp.int32, (tok, tok), 0)
            row_at = lax.broadcasted_iota(jnp.int32, (tok, tok), 1)
            same = same & (key_at <= row_at)
        bias_scr[at * tok : (at + 1) * tok, :] = jnp.where(same, 0.0, HIDDEN)

    def one_kv_head(j):
        cols = pl.ds(pl.multiple_of(j * HEAD_DIM, HEAD_DIM), HEAD_DIM)
        keys = jnp.concatenate([ref[:tok, cols] for ref in pieces], axis=0)
        values = jnp.concatenate([ref[tok : 2 * tok, cols] for ref in pieces], axis=0)
        keys_t = jnp.concatenate([ref[:tok, cols].T for ref in pieces], axis=1)

        def head_cols(h):
            return pl.ds(pl.multiple_of((j * group + h) * HEAD_DIM, HEAD_DIM), HEAD_DIM)

        bias = bias_scr[...]
        for pair in range(group // 2):
            q2 = jnp.concatenate([q_ref[:, head_cols(2 * pair + i)] for i in range(2)], axis=0)
            g2 = jnp.concatenate([g_ref[:, head_cols(2 * pair + i)] for i in range(2)], axis=0)
            d2 = jnp.concatenate([delta_ref[pl.ds(j * group + 2 * pair + i, 1), :] for i in range(2)], axis=1)
            s = dot(keys, q2, NT) + jnp.concatenate([bias, bias], axis=1)
            top = jnp.max(s, axis=0, keepdims=True)
            e = jnp.exp2((s - top) * LOG2_SCALE)
            prob = e * (1.0 / jnp.sum(e, axis=0, keepdims=True))
            dprob = dot(values, g2, NT)
            at = slice(2 * pair * tok, 2 * (pair + 1) * tok)
            p_scr[:, at] = prob.astype(jnp.bfloat16)
            ds_scr[:, at] = (prob * (dprob - d2)).astype(jnp.bfloat16)
        q_all = jnp.concatenate([q_ref[:, head_cols(h)] for h in range(group)], axis=0)
        g_all = jnp.concatenate([g_ref[:, head_cols(h)] for h in range(group)], axis=0)
        dk = dot(ds_scr[...], q_all, NN) * SCALE
        dv = dot(p_scr[...], g_all, NN)
        for at, out in enumerate(outs):
            out[:tok, cols] = dk[at * tok : (at + 1) * tok].astype(out.dtype)
            out[tok : 2 * tok, cols] = dv[at * tok : (at + 1) * tok].astype(out.dtype)
        dq_t = dot(keys_t, ds_scr[...], NN) * SCALE
        for h in range(group):
            dq_ref[:, head_cols(h)] = dq_t[:, h * tok : (h + 1) * tok].T.astype(jnp.bfloat16)

    lax.fori_loop(0, kv_heads, lambda j, c: (one_kv_head(j), c)[1], 0)


def attention(query, out_grad, delta, own, b1, a1, b2, a2, group, chunk, chunks):
    tok = query.shape[0]
    width = own.shape[1]
    kv_heads = width // HEAD_DIM
    wide = kv_heads * group * HEAD_DIM
    ext = MOST + tok
    whole = lambda a: pl.BlockSpec(a.shape, lambda i: (0, 0))
    pending = jax.ShapeDtypeStruct((2 * tok, width), jnp.bfloat16)
    out_shape = (
        jax.ShapeDtypeStruct((tok, wide), jnp.bfloat16),
        jax.ShapeDtypeStruct((2 * tok, width), jnp.float32),
        pending, pending, pending, pending,
    )
    return pl.pallas_call(
        functools.partial(attention_kernel, tok, group, kv_heads),
        grid=(1,),
        in_specs=[
            pl.BlockSpec((tok, wide), lambda i: (0, chunk)),
            pl.BlockSpec((tok, wide), lambda i: (0, chunk)),
            pl.BlockSpec((kv_heads * group, tok), lambda i: (chunk, 0)),
        ] + [whole(own)] * 5,
        out_specs=tuple(whole(o) for o in out_shape),
        out_shape=out_shape,
        scratch_shapes=[
            pltpu.VMEM((ext, tok), jnp.float32),
            pltpu.VMEM((ext, group * tok), jnp.bfloat16),
            pltpu.VMEM((ext, group * tok), jnp.bfloat16),
        ],
        compiler_params=pltpu.CompilerParams(vmem_limit_bytes=48 * 2**20),
        cost_estimate=pl.CostEstimate(
            flops=10 * ext * tok * kv_heads * group * HEAD_DIM,
            bytes_accessed=6 * tok * wide + 12 * ext * width,
            transcendentals=ext * tok * kv_heads * group,
        ),
        name="attention_backward",
    )(query, out_grad, delta, own, b1, a1, b2, a2)


def per_device(query, key, value, attn_out, out_grad, segments):
    tok = query.shape[0]
    heads = query.shape[1] // HEAD_DIM
    kv_heads = key.shape[1] // HEAD_DIM
    group = heads // kv_heads
    width = key.shape[1] // CHUNKS
    odd = lax.axis_index("head") % 2 == 1
    documents = jnp.tile((segments + 1).astype(jnp.bfloat16)[None, :], (16, width // tok))
    delta = row_delta(out_grad, attn_out)
    dq_parts, dk_parts, dv_parts = [], [], []
    for c in range(CHUNKS):
        cols = slice(c * width, (c + 1) * width)
        own = jnp.concatenate([key[:, cols], value[:, cols], documents], axis=0)
        a1 = shift(own, 2)
        a2 = shift(a1, 2)
        b1 = swap(jnp.where(odd, a1, own))
        b2 = swap(jnp.where(odd, a2, a1))
        dq, mine, d1, d2, d3, d4 = attention(query, out_grad, delta, own, b1, a1, b2, a2, group, c, CHUNKS)
        c3 = swap(d3)
        c1 = swap(d1)
        add = lambda *terms: sum(t.astype(jnp.float32) for t in terms)
        zero = jnp.zeros_like(c1)
        far = add(d4, jnp.where(odd, c3, zero)).astype(jnp.bfloat16)
        e1 = shift(far, -2)
        near = add(d2, jnp.where(odd, c1, c3), e1).astype(jnp.bfloat16)
        e2 = shift(near, -2)
        total = add(mine, jnp.where(odd, zero, c1), e2).astype(jnp.bfloat16)
        dq_parts.append(dq)
        dk_parts.append(total[:tok])
        dv_parts.append(total[tok:])
    join = lambda parts: parts[0] if len(parts) == 1 else jnp.concatenate(parts, axis=1)
    return join(dq_parts), join(dk_parts), join(dv_parts)


def solution(mesh):
    split = P(AXES, None)
    return jax.shard_map(
        per_device,
        mesh=mesh,
        in_specs=(split, split, split, split, split, P(AXES)),
        out_specs=(split, split, split),
        check_vma=False,
    )
```

```python
import functools
import math

import jax
import jax.numpy as jnp
from jax import lax
from jax.experimental import pallas as pl
from jax.experimental.pallas import tpu as pltpu
from jax.sharding import PartitionSpec as P

HEAD_DIM = 128
MOST = 512
LOG2_SCALE = HEAD_DIM ** (-0.5) * math.log2(math.e)
SCALE = HEAD_DIM ** (-0.5)
HIDDEN = -1e30
AXES = ("ctx", "head")
NT = (((1,), (1,)), ((), ()))
NN = (((1,), (0,)), ((), ()))


def shift(value, steps):
    count = lax.axis_size(AXES)
    return lax.ppermute(value, AXES, [(i, i + steps) for i in range(count) if 0 <= i + steps < count])


def dot(a, b, dims):
    return lax.dot_general(a, b, dims, preferred_element_type=jnp.float32)


def head_cols(h):
    return pl.ds(pl.multiple_of(h * HEAD_DIM, HEAD_DIM), HEAD_DIM)


def fill_bias(bias_scr, own_ref, pieces, tok):
    def documents(ref):
        rows = ref[2 * tok : 2 * tok + 16, :tok].astype(jnp.float32)
        return jnp.concatenate([rows] * (tok // 16), axis=0)

    mine = documents(own_ref)
    for at, ref in enumerate(pieces):
        same = documents(ref).T == mine
        if ref is own_ref:
            key_at = lax.broadcasted_iota(jnp.int32, (tok, tok), 0)
            row_at = lax.broadcasted_iota(jnp.int32, (tok, tok), 1)
            same = same & (key_at <= row_at)
        bias_scr[at * tok : (at + 1) * tok, :] = jnp.where(same, 0.0, HIDDEN)


def stack(pieces, rows, cols):
    return jnp.concatenate([ref[rows, cols] for ref in pieces], axis=0)


def pair_rows(ref, first):
    return jnp.concatenate([ref[:, head_cols(first + i)] for i in range(2)], axis=0)


def pair_stat(ref, first):
    return jnp.concatenate([ref[pl.ds(first + i, 1), :] for i in range(2)], axis=1)


def put_stat(ref, first, value):
    tok = ref.shape[1]
    for i in range(2):
        ref[pl.ds(first + i, 1), :] = value[:, i * tok : (i + 1) * tok]


def near_stats_kernel(tok, group, kv_heads, q_ref, g_ref, o_ref, own_ref, r1_ref, r2_ref, top_ref, sum_ref, delta_ref, bias_scr):
    pieces = (r2_ref, r1_ref, own_ref)
    fill_bias(bias_scr, own_ref, pieces, tok)

    def one_kv_head(j, carry):
        keys = stack(pieces, slice(0, tok), head_cols(j))
        for pair in range(group // 2):
            first = j * group + 2 * pair
            bias = bias_scr[...]
            s = dot(keys, pair_rows(q_ref, first), NT) + jnp.concatenate([bias, bias], axis=1)
            top = jnp.max(s, axis=0, keepdims=True)
            put_stat(top_ref, first, top)
            put_stat(sum_ref, first, jnp.sum(jnp.exp2((s - top) * LOG2_SCALE), axis=0, keepdims=True))
            prod = pair_rows(g_ref, first).astype(jnp.float32) * pair_rows(o_ref, first).astype(jnp.float32)
            put_stat(delta_ref, first, jnp.sum(prod.T, axis=0, keepdims=True))
        return carry

    lax.fori_loop(0, kv_heads, one_kv_head, 0)


def gradients(ds, p, q_ref, g_ref, j, group):
    q_all = jnp.concatenate([q_ref[:, head_cols(j * group + h)] for h in range(group)], axis=0)
    g_all = jnp.concatenate([g_ref[:, head_cols(j * group + h)] for h in range(group)], axis=0)
    return dot(ds, q_all, NN) * SCALE, dot(p, g_all, NN)


def put_gradients(outs, dk, dv, j, tok):
    for at, out in enumerate(outs):
        out[:tok, head_cols(j)] = dk[at * tok : (at + 1) * tok].astype(out.dtype)
        out[tok : 2 * tok, head_cols(j)] = dv[at * tok : (at + 1) * tok].astype(out.dtype)


def far_kernel(
    tok, group, kv_heads,
    q_ref, g_ref, own_ref, r3_ref, r4_ref, near_top_ref, near_sum_ref, delta_ref,
    d3_ref, d4_ref, top_ref, inv_ref, ds_ref,
    bias_scr, p_scr,
):
    pieces = (r4_ref, r3_ref)
    fill_bias(bias_scr, own_ref, pieces, tok)

    def one_kv_head(j, carry):
        keys = stack(pieces, slice(0, tok), head_cols(j))
        values = stack(pieces, slice(tok, 2 * tok), head_cols(j))
        for pair in range(group // 2):
            first = j * group + 2 * pair
            bias = bias_scr[...]
            s = dot(keys, pair_rows(q_ref, first), NT) + jnp.concatenate([bias, bias], axis=1)
            near_top = pair_stat(near_top_ref, first)
            top = jnp.maximum(near_top, jnp.max(s, axis=0, keepdims=True))
            e = jnp.exp2((s - top) * LOG2_SCALE)
            total = pair_stat(near_sum_ref, first) * jnp.exp2((near_top - top) * LOG2_SCALE) + jnp.sum(e, axis=0, keepdims=True)
            inv = 1.0 / total
            put_stat(top_ref, first, top)
            put_stat(inv_ref, first, inv)
            prob = e * inv
            dprob = dot(values, pair_rows(g_ref, first), NT)
            p_scr[:, 2 * pair * tok : 2 * (pair + 1) * tok] = prob.astype(jnp.bfloat16)
            low = (prob * (dprob - pair_stat(delta_ref, first))).astype(jnp.bfloat16)
            for i in range(2):
                ds_ref[:, head_cols(first + i)] = low[:, i * tok : (i + 1) * tok]
        cols = pl.ds(pl.multiple_of(j * group * HEAD_DIM, HEAD_DIM), group * HEAD_DIM)
        dk, dv = gradients(ds_ref[:, cols], p_scr[...], q_ref, g_ref, j, group)
        put_gradients((d4_ref, d3_ref), dk, dv, j, tok)
        return carry

    lax.fori_loop(0, kv_heads, one_kv_head, 0)


def near_kernel(
    tok, group, kv_heads,
    q_ref, g_ref, own_ref, r1_ref, r2_ref, r3_ref, r4_ref, top_ref, inv_ref, delta_ref, far_ds_ref,
    dq_ref, own_out, d1_ref, d2_ref,
    bias_scr, p_scr, ds_scr,
):
    pieces = (r2_ref, r1_ref, own_ref)
    fill_bias(bias_scr, own_ref, pieces, tok)

    def one_kv_head(j, carry):
        keys = stack(pieces, slice(0, tok), head_cols(j))
        values = stack(pieces, slice(tok, 2 * tok), head_cols(j))
        every = (r4_ref, r3_ref) + pieces
        keys_t = jnp.concatenate([ref[:tok, head_cols(j)].T for ref in every], axis=1)
        for pair in range(group // 2):
            first = j * group + 2 * pair
            bias = bias_scr[...]
            s = dot(keys, pair_rows(q_ref, first), NT) + jnp.concatenate([bias, bias], axis=1)
            prob = jnp.exp2((s - pair_stat(top_ref, first)) * LOG2_SCALE) * pair_stat(inv_ref, first)
            dprob = dot(values, pair_rows(g_ref, first), NT)
            at = slice(2 * pair * tok, 2 * (pair + 1) * tok)
            p_scr[:, at] = prob.astype(jnp.bfloat16)
            ds_scr[:, at] = (prob * (dprob - pair_stat(delta_ref, first))).astype(jnp.bfloat16)
        dk, dv = gradients(ds_scr[...], p_scr[...], q_ref, g_ref, j, group)
        put_gradients((d2_ref, d1_ref, own_out), dk, dv, j, tok)
        cols = pl.ds(pl.multiple_of(j * group * HEAD_DIM, HEAD_DIM), group * HEAD_DIM)
        ds_all = jnp.concatenate([far_ds_ref[:, cols], ds_scr[...]], axis=0)
        dq_t = dot(keys_t, ds_all, NN) * SCALE
        for h in range(group):
            dq_ref[:, head_cols(j * group + h)] = dq_t[:, h * tok : (h + 1) * tok].T.astype(jnp.bfloat16)
        return carry

    lax.fori_loop(0, kv_heads, one_kv_head, 0)


def call(kernel, name, args, out_shape, scratch, keys, products, sizes):
    tok, group, kv_heads = sizes
    whole = pl.BlockSpec(memory_space=pltpu.VMEM)
    pairs = keys * tok * group * kv_heads
    return pl.pallas_call(
        functools.partial(kernel, *sizes),
        in_specs=[whole] * len(args),
        out_specs=tuple(whole for _ in out_shape),
        out_shape=tuple(jax.ShapeDtypeStruct(s, d) for s, d in out_shape),
        scratch_shapes=[pltpu.VMEM(s, d) for s, d in scratch],
        compiler_params=pltpu.CompilerParams(vmem_limit_bytes=40 * 2**20),
        cost_estimate=pl.CostEstimate(
            flops=2 * products * pairs * HEAD_DIM, bytes_accessed=sum(a.size * a.dtype.itemsize for a in args), transcendentals=pairs
        ),
        name=name,
    )(*args)


def per_device(query, key, value, attn_out, out_grad, segments):
    tok = query.shape[0]
    heads = query.shape[1] // HEAD_DIM
    width = key.shape[1]
    kv_heads = width // HEAD_DIM
    group = heads // kv_heads
    sizes = (tok, group, kv_heads)
    f32, bf16 = jnp.float32, jnp.bfloat16
    documents = jnp.tile((segments + 1).astype(bf16)[None, :], (16, width // tok))
    own = jnp.concatenate([key, value, documents], axis=0)
    r2 = shift(own, 2)
    r1 = shift(own, 1)
    r4 = shift(r2, 2)
    r3 = shift(r1, 2)
    stat = ((heads, tok), f32)
    pending = ((2 * tok, width), bf16)
    near, far = 3 * tok, 2 * tok
    near_top, near_sum, delta = call(
        near_stats_kernel, "near_stats", (query, out_grad, attn_out, own, r1, r2),
        (stat, stat, stat), (((near, tok), f32),), near, 1, sizes,
    )
    d3, d4, top, inv, far_ds = call(
        far_kernel, "far_gradients", (query, out_grad, own, r3, r4, near_top, near_sum, delta),
        (pending, pending, stat, stat, ((far, heads * tok), bf16)),
        (((far, tok), f32), ((far, group * tok), bf16)), far, 4, sizes,
    )
    x4 = shift(d4, -2)
    x3 = shift(d3, -2)
    query_grad, mine, d1, d2 = call(
        near_kernel, "near_gradients", (query, out_grad, own, r1, r2, r3, r4, top, inv, delta, far_ds),
        (((tok, heads * HEAD_DIM), bf16), ((2 * tok, width), f32), pending, pending),
        (((near, tok), f32), ((near, group * tok), bf16), ((near, group * tok), bf16)), near, 5, sizes,
    )
    y2 = shift((d2.astype(f32) + x4.astype(f32)).astype(bf16), -2)
    y1 = shift((d1.astype(f32) + x3.astype(f32)).astype(bf16), -1)
    total = (mine + y2.astype(f32) + y1.astype(f32)).astype(bf16)
    return query_grad, total[:tok], total[tok:]


def solution(mesh):
    split = P(AXES, None)
    return jax.shard_map(
        per_device,
        mesh=mesh,
        in_specs=(split, split, split, split, split, P(AXES)),
        out_specs=(split, split, split),
        check_vma=False,
    )
```

```python
import functools
import math

import jax
import jax.numpy as jnp
from jax import lax
from jax.experimental import pallas as pl
from jax.experimental.pallas import tpu as pltpu
from jax.sharding import PartitionSpec as P

HEAD_DIM = 128
MOST = 512
CHUNKS = 2
FULL1 = False
FULL2 = False
EARLY = True
LOG2_SCALE = HEAD_DIM ** (-0.5) * math.log2(math.e)
SCALE = HEAD_DIM ** (-0.5)
HIDDEN = -1e30
AXES = ("ctx", "head")
NT = (((1,), (1,)), ((), ()))
NN = (((1,), (0,)), ((), ()))


def shift(value, steps):
    count = lax.axis_size(AXES)
    return lax.ppermute(value, AXES, [(i, i + steps) for i in range(count) if 0 <= i + steps < count])


def dot(a, b, dims):
    return lax.dot_general(a, b, dims, preferred_element_type=jnp.float32)


def head_cols(h):
    return pl.ds(pl.multiple_of(h * HEAD_DIM, HEAD_DIM), HEAD_DIM)


def fill_bias(bias_scr, own, pieces, tok):
    def documents(piece):
        ref, base = piece
        rows = ref[base + 2 * tok : base + 2 * tok + 16, :tok].astype(jnp.float32)
        return jnp.concatenate([rows] * (tok // 16), axis=0)

    mine = documents(own)
    for at, piece in enumerate(pieces):
        same = documents(piece).T == mine
        if piece is own:
            key_at = lax.broadcasted_iota(jnp.int32, (tok, tok), 0)
            row_at = lax.broadcasted_iota(jnp.int32, (tok, tok), 1)
            same = same & (key_at <= row_at)
        bias_scr[at * tok : (at + 1) * tok, :] = jnp.where(same, 0.0, HIDDEN)


def stack(pieces, start, tok, cols):
    return jnp.concatenate([ref[base + start : base + start + tok, cols] for ref, base in pieces], axis=0)


def pair_rows(ref, first):
    return jnp.concatenate([ref[:, head_cols(first + i)] for i in range(2)], axis=0)


def pair_stat(ref, first):
    return jnp.concatenate([ref[pl.ds(first + i, 1), :] for i in range(2)], axis=1)


def put_stat(ref, first, value):
    tok = ref.shape[1]
    for i in range(2):
        ref[pl.ds(first + i, 1), :] = value[:, i * tok : (i + 1) * tok]


def near_stats_kernel(tok, group, kv_heads, offset, q_ref, g_ref, o_ref, own_ref, r1_ref, r2_ref, top_ref, sum_ref, delta_ref, bias_scr):
    own = (own_ref, 0)
    pieces = ((r2_ref, 0), (r1_ref, 0), own)
    fill_bias(bias_scr, own, pieces, tok)

    def one_kv_head(j, carry):
        keys = stack(pieces, 0, tok, head_cols(j))
        for pair in range(group // 2):
            first = j * group + 2 * pair
            bias = bias_scr[...]
            s = dot(keys, pair_rows(q_ref, offset + first), NT) + jnp.concatenate([bias, bias], axis=1)
            top = jnp.max(s, axis=0, keepdims=True)
            put_stat(top_ref, first, top)
            put_stat(sum_ref, first, jnp.sum(jnp.exp2((s - top) * LOG2_SCALE), axis=0, keepdims=True))
            prod = pair_rows(g_ref, offset + first).astype(jnp.float32) * pair_rows(o_ref, offset + first).astype(jnp.float32)
            put_stat(delta_ref, first, jnp.sum(prod.T, axis=0, keepdims=True))
        return carry

    lax.fori_loop(0, kv_heads, one_kv_head, 0, unroll=True)


def gradients(ds, p, q_ref, g_ref, first, group):
    q_all = jnp.concatenate([q_ref[:, head_cols(first + h)] for h in range(group)], axis=0)
    g_all = jnp.concatenate([g_ref[:, head_cols(first + h)] for h in range(group)], axis=0)
    return dot(ds, q_all, NN) * SCALE, dot(p, g_all, NN)


def put_gradients(outs, dk, dv, j, tok):
    for at, (out, base) in enumerate(outs):
        out[base : base + tok, head_cols(j)] = dk[at * tok : (at + 1) * tok].astype(out.dtype)
        out[base + tok : base + 2 * tok, head_cols(j)] = dv[at * tok : (at + 1) * tok].astype(out.dtype)


def far_kernel(
    tok, group, kv_heads, offset,
    q_ref, g_ref, own_ref, far_ref, near_top_ref, near_sum_ref, delta_ref,
    d43_ref, lse_ref, ds_ref,
    bias_scr, p_scr,
):
    pieces = ((far_ref, 0), (far_ref, far_ref.shape[0] // 2))
    fill_bias(bias_scr, (own_ref, 0), pieces, tok)

    def one_kv_head(j, carry):
        keys = stack(pieces, 0, tok, head_cols(j))
        values = stack(pieces, tok, tok, head_cols(j))
        for pair in range(group // 2):
            first = j * group + 2 * pair
            bias = bias_scr[...]
            s = dot(keys, pair_rows(q_ref, offset + first), NT) + jnp.concatenate([bias, bias], axis=1)
            near_top = pair_stat(near_top_ref, first)
            top = jnp.maximum(near_top, jnp.max(s, axis=0, keepdims=True))
            e = jnp.exp2((s - top) * LOG2_SCALE)
            total = pair_stat(near_sum_ref, first) * jnp.exp2((near_top - top) * LOG2_SCALE) + jnp.sum(e, axis=0, keepdims=True)
            inv = 1.0 / total
            put_stat(lse_ref, first, top * LOG2_SCALE + jnp.log2(total))
            prob = e * inv
            dprob = dot(values, pair_rows(g_ref, offset + first), NT)
            p_scr[:, 2 * pair * tok : 2 * (pair + 1) * tok] = prob.astype(jnp.bfloat16)
            low = (prob * (dprob - pair_stat(delta_ref, first))).astype(jnp.bfloat16)
            for i in range(2):
                ds_ref[:, head_cols(first + i)] = low[:, i * tok : (i + 1) * tok]
        cols = pl.ds(pl.multiple_of(j * group * HEAD_DIM, HEAD_DIM), group * HEAD_DIM)
        dk, dv = gradients(ds_ref[:, cols], p_scr[...], q_ref, g_ref, offset + j * group, group)
        put_gradients(((d43_ref, 0), (d43_ref, 2 * tok)), dk, dv, j, tok)
        return carry

    lax.fori_loop(0, kv_heads, one_kv_head, 0, unroll=True)


def middle_kernel(
    tok, group, kv_heads, offset,
    q_ref, g_ref, own_ref, r1_ref, r2_ref, lse_ref, delta_ref,
    d2_ref, d1_ref, ds_ref,
    bias_scr, p_scr,
):
    pieces = ((r2_ref, 0), (r1_ref, 0))
    fill_bias(bias_scr, (own_ref, 0), pieces, tok)

    def one_kv_head(j, carry):
        scores_gradient(pieces, bias_scr, p_scr, ds_ref, q_ref, g_ref, lse_ref, delta_ref, j, tok, group, offset)
        cols = pl.ds(pl.multiple_of(j * group * HEAD_DIM, HEAD_DIM), group * HEAD_DIM)
        dk, dv = gradients(ds_ref[:, cols], p_scr[...], q_ref, g_ref, offset + j * group, group)
        put_gradients(((d2_ref, 0), (d1_ref, 0)), dk, dv, j, tok)
        return carry

    lax.fori_loop(0, kv_heads, one_kv_head, 0, unroll=True)


def scores_gradient(pieces, bias_scr, p_scr, ds_ref, q_ref, g_ref, lse_ref, delta_ref, j, tok, group, offset):
    keys = stack(pieces, 0, tok, head_cols(j))
    values = stack(pieces, tok, tok, head_cols(j))
    for pair in range(group // 2):
        first = j * group + 2 * pair
        bias = bias_scr[...]
        s = dot(keys, pair_rows(q_ref, offset + first), NT) + jnp.concatenate([bias, bias], axis=1)
        prob = jnp.exp2(s * LOG2_SCALE - pair_stat(lse_ref, first))
        dprob = dot(values, pair_rows(g_ref, offset + first), NT)
        p_scr[:, 2 * pair * tok : 2 * (pair + 1) * tok] = prob.astype(jnp.bfloat16)
        low = (prob * (dprob - pair_stat(delta_ref, first))).astype(jnp.bfloat16)
        for i in range(2):
            ds_ref[:, head_cols(first + i)] = low[:, i * tok : (i + 1) * tok]


def own_kernel(
    tok, group, kv_heads, offset,
    q_ref, g_ref, own_ref, r1_ref, r2_ref, far_ref, lse_ref, delta_ref, far_ds_ref, middle_ds_ref,
    dq_ref, own_out,
    bias_scr, p_scr, ds_scr,
):
    own = (own_ref, 0)
    fill_bias(bias_scr, own, (own,), tok)

    def one_kv_head(j, carry):
        scores_gradient((own,), bias_scr, p_scr, ds_scr, q_ref, g_ref, lse_ref, delta_ref, j, tok, group, offset)
        cols = pl.ds(pl.multiple_of(j * group * HEAD_DIM, HEAD_DIM), group * HEAD_DIM)
        dk, dv = gradients(ds_scr[:, cols], p_scr[...], q_ref, g_ref, offset + j * group, group)
        put_gradients(((own_out, 0),), dk, dv, j, tok)
        every = ((far_ref, 0), (far_ref, far_ref.shape[0] // 2), (r2_ref, 0), (r1_ref, 0), own)
        keys_t = jnp.concatenate([ref[base : base + tok, head_cols(j)].T for ref, base in every], axis=1)
        ds_all = jnp.concatenate([far_ds_ref[:, cols], middle_ds_ref[:, cols], ds_scr[:, cols]], axis=0)
        dq_t = dot(keys_t, ds_all, NN) * SCALE
        for h in range(group):
            dq_ref[:, head_cols(j * group + h)] = dq_t[:, h * tok : (h + 1) * tok].T.astype(jnp.bfloat16)
        return carry

    lax.fori_loop(0, kv_heads, one_kv_head, 0, unroll=True)


def call(kernel, name, args, out_shape, scratch, keys, products, sizes):
    tok, group, kv_heads, _ = sizes
    whole = pl.BlockSpec(memory_space=pltpu.VMEM)
    pairs = keys * tok * group * kv_heads
    return pl.pallas_call(
        functools.partial(kernel, *sizes),
        in_specs=[whole] * len(args),
        out_specs=tuple(whole for _ in out_shape),
        out_shape=tuple(jax.ShapeDtypeStruct(s, d) for s, d in out_shape),
        scratch_shapes=[pltpu.VMEM(s, d) for s, d in scratch],
        compiler_params=pltpu.CompilerParams(vmem_limit_bytes=40 * 2**20),
        cost_estimate=pl.CostEstimate(
            flops=2 * products * pairs * HEAD_DIM, bytes_accessed=sum(a.size * a.dtype.itemsize for a in args), transcendentals=pairs
        ),
        name=name,
    )(*args)


def per_device(query, key, value, attn_out, out_grad, segments):
    tok = query.shape[0]
    heads = query.shape[1] // HEAD_DIM // CHUNKS
    width = key.shape[1] // CHUNKS
    kv_heads = width // HEAD_DIM
    group = heads // kv_heads
    f32, bf16 = jnp.float32, jnp.bfloat16
    documents = jnp.tile((segments + 1).astype(bf16)[None, :], (16, width // tok))
    stat = ((heads, tok), f32)
    near, far = 3 * tok, 2 * tok
    parts = range(CHUNKS)
    sizes = [(tok, group, kv_heads, c * heads) for c in parts]
    cols = [slice(c * width, (c + 1) * width) for c in parts]
    if FULL1:
        whole_own = jnp.concatenate([key, value, jnp.tile(documents, (1, CHUNKS))], axis=0)
        whole_r2 = shift(whole_own, 2)
        whole_r1 = shift(whole_own, 1)
        own, r2, r1 = ([a[:, cols[c]] for c in parts] for a in (whole_own, whole_r2, whole_r1))
    else:
        own = [jnp.concatenate([key[:, cols[c]], value[:, cols[c]], documents], axis=0) for c in parts]
        r2 = [shift(own[c], 2) for c in parts]
        r1 = [shift(own[c], 1) for c in parts]
    near_out, r43 = [], []
    for c in parts:
        relayed = jnp.concatenate([r2[c], r1[c]], axis=0)
        if near_out and EARLY:
            relayed, _ = lax.optimization_barrier((relayed, near_out[-1]))
        r43.append(shift(relayed, 2))
        near_out.append(call(
            near_stats_kernel, "near_stats", (query, out_grad, attn_out, own[c], r1[c], r2[c]),
            (stat, stat, stat), (((near, tok), f32),), near, 1, sizes[c],
        ))
    pending = ((2 * tok, width), bf16)
    saved = ((far, heads * tok), bf16)
    far_out, x43 = [], []
    for c in parts:
        near_top, near_sum, delta = near_out[c]
        far_out.append(call(
            far_kernel, "far_gradients", (query, out_grad, own[c], r43[c], near_top, near_sum, delta),
            (((4 * tok, width), bf16), stat, saved),
            (((far, tok), f32), ((far, group * tok), bf16)), far, 4, sizes[c],
        ))
        x43.append(shift(far_out[c][0], -2))
    sums, middle_ds = [], []
    for c in parts:
        lse = far_out[c][1]
        if sums and not FULL2:
            lse, _ = lax.optimization_barrier((lse, sums[-1]))
        d2, d1, ds = call(
            middle_kernel, "near_middle", (query, out_grad, own[c], r1[c], r2[c], lse, near_out[c][2]),
            (pending, pending, saved), (((far, tok), f32), ((far, group * tok), bf16)), far, 4, sizes[c],
        )
        middle_ds.append(ds)
        sums.append((
            (d2.astype(f32) + x43[c][: 2 * tok].astype(f32)).astype(bf16),
            (d1.astype(f32) + x43[c][2 * tok :].astype(f32)).astype(bf16),
        ))
    if FULL2:
        sums = [tuple(jnp.concatenate(a, axis=1) for a in zip(*sums))]
        sums = lax.optimization_barrier(sums)
    back = [(shift(sum2, -2), shift(sum1, -1)) for sum2, sum1 in sums]
    dq, mine = [], []
    for c in parts:
        lse, _ = lax.optimization_barrier((far_out[c][1], sums[-1]))
        query_grad, terms = call(
            own_kernel, "near_own",
            (query, out_grad, own[c], r1[c], r2[c], r43[c], lse, near_out[c][2], far_out[c][2], middle_ds[c]),
            (((tok, heads * HEAD_DIM), bf16), ((2 * tok, width), f32)),
            (((tok, tok), f32), ((tok, group * tok), bf16), ((tok, heads * tok), bf16)), tok, 9, sizes[c],
        )
        dq.append(query_grad)
        mine.append(terms)
    if FULL2:
        mine = [jnp.concatenate(mine, axis=1)]
    total = [(m + y2.astype(f32) + y1.astype(f32)).astype(bf16) for m, (y2, y1) in zip(mine, back)]
    total = lax.optimization_barrier(jnp.concatenate(total, axis=1))
    return jnp.concatenate(dq, axis=1), total[:tok], total[tok:]


def solution(mesh):
    split = P(AXES, None)
    return jax.shard_map(
        per_device,
        mesh=mesh,
        in_specs=(split, split, split, split, split, P(AXES)),
        out_specs=(split, split, split),
        check_vma=False,
    )
```

```python
import functools
import math

import jax
import jax.numpy as jnp
from jax import lax
from jax.experimental import pallas as pl
from jax.experimental.pallas import tpu as pltpu
from jax.sharding import PartitionSpec as P

HEAD_DIM = 128
MOST = 512
CHUNKS = 2
FULL1 = False
FULL2 = False
EARLY = True
LOG2_SCALE = HEAD_DIM ** (-0.5) * math.log2(math.e)
SCALE = HEAD_DIM ** (-0.5)
HIDDEN = -1e30
AXES = ("ctx", "head")
NT = (((1,), (1,)), ((), ()))
NN = (((1,), (0,)), ((), ()))


def shift(value, steps):
    count = lax.axis_size(AXES)
    return lax.ppermute(value, AXES, [(i, i + steps) for i in range(count) if 0 <= i + steps < count])


def dot(a, b, dims):
    return lax.dot_general(a, b, dims, preferred_element_type=jnp.float32)


def head_cols(h):
    return pl.ds(pl.multiple_of(h * HEAD_DIM, HEAD_DIM), HEAD_DIM)


def fill_bias(bias_scr, own, pieces, tok):
    def documents(piece):
        ref, base = piece
        rows = ref[base + 2 * tok : base + 2 * tok + 16, :tok].astype(jnp.float32)
        return jnp.concatenate([rows] * (tok // 16), axis=0)

    mine = documents(own)
    for at, piece in enumerate(pieces):
        same = documents(piece).T == mine
        if piece is own:
            key_at = lax.broadcasted_iota(jnp.int32, (tok, tok), 0)
            row_at = lax.broadcasted_iota(jnp.int32, (tok, tok), 1)
            same = same & (key_at <= row_at)
        bias_scr[at * tok : (at + 1) * tok, :] = jnp.where(same, 0.0, HIDDEN)


def stack(pieces, start, tok, cols):
    return jnp.concatenate([ref[base + start : base + start + tok, cols] for ref, base in pieces], axis=0)


def pair_rows(ref, first):
    return jnp.concatenate([ref[:, head_cols(first + i)] for i in range(2)], axis=0)


def pair_stat(ref, first):
    return jnp.concatenate([ref[pl.ds(first + i, 1), :] for i in range(2)], axis=1)


def put_stat(ref, first, value):
    tok = ref.shape[1]
    for i in range(2):
        ref[pl.ds(first + i, 1), :] = value[:, i * tok : (i + 1) * tok]


def near_stats_kernel(tok, group, kv_heads, offset, q_ref, g_ref, o_ref, own_ref, r1_ref, r2_ref, top_ref, sum_ref, *rest):
    *delta_refs, bias_scr = rest
    own = (own_ref, 0)
    pieces = ((r2_ref, 0), (r1_ref, 0), own)
    fill_bias(bias_scr, own, pieces, tok)

    def one_kv_head(j, carry):
        keys = stack(pieces, 0, tok, head_cols(j))
        for pair in range(group // 2):
            first = j * group + 2 * pair
            bias = bias_scr[...]
            s = dot(keys, pair_rows(q_ref, offset + first), NT) + jnp.concatenate([bias, bias], axis=1)
            top = jnp.max(s, axis=0, keepdims=True)
            put_stat(top_ref, first, top)
            put_stat(sum_ref, first, jnp.sum(jnp.exp2((s - top) * LOG2_SCALE), axis=0, keepdims=True))
        return carry

    lax.fori_loop(0, kv_heads, one_kv_head, 0, unroll=True)
    for c, delta_ref in enumerate(delta_refs):
        heads = delta_ref.shape[0]
        for first in range(0, heads, 2):
            head = c * heads + first
            prod = pair_rows(g_ref, head).astype(jnp.float32) * pair_rows(o_ref, head).astype(jnp.float32)
            put_stat(delta_ref, first, jnp.sum(prod.T, axis=0, keepdims=True))


def gradients(ds, p, q_ref, g_ref, first, group):
    q_all = jnp.concatenate([q_ref[:, head_cols(first + h)] for h in range(group)], axis=0)
    g_all = jnp.concatenate([g_ref[:, head_cols(first + h)] for h in range(group)], axis=0)
    return dot(ds, q_all, NN) * SCALE, dot(p, g_all, NN)


def put_gradients(outs, dk, dv, j, tok):
    for at, (out, base) in enumerate(outs):
        out[base : base + tok, head_cols(j)] = dk[at * tok : (at + 1) * tok].astype(out.dtype)
        out[base + tok : base + 2 * tok, head_cols(j)] = dv[at * tok : (at + 1) * tok].astype(out.dtype)


def far_kernel(
    tok, group, kv_heads, offset,
    q_ref, g_ref, own_ref, far_ref, near_top_ref, near_sum_ref, delta_ref,
    d43_ref, lse_ref, ds_ref,
    bias_scr, p_scr,
):
    pieces = ((far_ref, 0), (far_ref, far_ref.shape[0] // 2))
    fill_bias(bias_scr, (own_ref, 0), pieces, tok)

    def one_kv_head(j, carry):
        keys = stack(pieces, 0, tok, head_cols(j))
        values = stack(pieces, tok, tok, head_cols(j))
        for pair in range(group // 2):
            first = j * group + 2 * pair
            bias = bias_scr[...]
            s = dot(keys, pair_rows(q_ref, offset + first), NT) + jnp.concatenate([bias, bias], axis=1)
            near_top = pair_stat(near_top_ref, first)
            top = jnp.maximum(near_top, jnp.max(s, axis=0, keepdims=True))
            e = jnp.exp2((s - top) * LOG2_SCALE)
            total = pair_stat(near_sum_ref, first) * jnp.exp2((near_top - top) * LOG2_SCALE) + jnp.sum(e, axis=0, keepdims=True)
            inv = 1.0 / total
            put_stat(lse_ref, first, top * LOG2_SCALE + jnp.log2(total))
            prob = e * inv
            dprob = dot(values, pair_rows(g_ref, offset + first), NT)
            p_scr[:, 2 * pair * tok : 2 * (pair + 1) * tok] = prob.astype(jnp.bfloat16)
            low = (prob * (dprob - pair_stat(delta_ref, first))).astype(jnp.bfloat16)
            for i in range(2):
                ds_ref[:, head_cols(first + i)] = low[:, i * tok : (i + 1) * tok]
        cols = pl.ds(pl.multiple_of(j * group * HEAD_DIM, HEAD_DIM), group * HEAD_DIM)
        dk, dv = gradients(ds_ref[:, cols], p_scr[...], q_ref, g_ref, offset + j * group, group)
        put_gradients(((d43_ref, 0), (d43_ref, 2 * tok)), dk, dv, j, tok)
        return carry

    lax.fori_loop(0, kv_heads, one_kv_head, 0, unroll=True)


def middle_kernel(
    tok, group, kv_heads, offset,
    q_ref, g_ref, own_ref, r1_ref, r2_ref, lse_ref, delta_ref,
    d2_ref, d1_ref, ds_ref,
    bias_scr, p_scr,
):
    pieces = ((r2_ref, 0), (r1_ref, 0))
    fill_bias(bias_scr, (own_ref, 0), pieces, tok)

    def one_kv_head(j, carry):
        scores_gradient(pieces, bias_scr, p_scr, ds_ref, q_ref, g_ref, lse_ref, delta_ref, j, tok, group, offset)
        cols = pl.ds(pl.multiple_of(j * group * HEAD_DIM, HEAD_DIM), group * HEAD_DIM)
        dk, dv = gradients(ds_ref[:, cols], p_scr[...], q_ref, g_ref, offset + j * group, group)
        put_gradients(((d2_ref, 0), (d1_ref, 0)), dk, dv, j, tok)
        return carry

    lax.fori_loop(0, kv_heads, one_kv_head, 0, unroll=True)


def scores_gradient(pieces, bias_scr, p_scr, ds_ref, q_ref, g_ref, lse_ref, delta_ref, j, tok, group, offset):
    keys = stack(pieces, 0, tok, head_cols(j))
    values = stack(pieces, tok, tok, head_cols(j))
    for pair in range(group // 2):
        first = j * group + 2 * pair
        bias = bias_scr[...]
        s = dot(keys, pair_rows(q_ref, offset + first), NT) + jnp.concatenate([bias, bias], axis=1)
        prob = jnp.exp2(s * LOG2_SCALE - pair_stat(lse_ref, first))
        dprob = dot(values, pair_rows(g_ref, offset + first), NT)
        p_scr[:, 2 * pair * tok : 2 * (pair + 1) * tok] = prob.astype(jnp.bfloat16)
        low = (prob * (dprob - pair_stat(delta_ref, first))).astype(jnp.bfloat16)
        for i in range(2):
            ds_ref[:, head_cols(first + i)] = low[:, i * tok : (i + 1) * tok]


def own_kernel(
    tok, group, kv_heads, offset,
    q_ref, g_ref, own_ref, r1_ref, r2_ref, far_ref, lse_ref, delta_ref, far_ds_ref, middle_ds_ref,
    dq_ref, own_out,
    bias_scr, p_scr, ds_scr,
):
    own = (own_ref, 0)
    fill_bias(bias_scr, own, (own,), tok)

    def one_kv_head(j, carry):
        scores_gradient((own,), bias_scr, p_scr, ds_scr, q_ref, g_ref, lse_ref, delta_ref, j, tok, group, offset)
        cols = pl.ds(pl.multiple_of(j * group * HEAD_DIM, HEAD_DIM), group * HEAD_DIM)
        dk, dv = gradients(ds_scr[:, cols], p_scr[...], q_ref, g_ref, offset + j * group, group)
        put_gradients(((own_out, 0),), dk, dv, j, tok)
        every = ((far_ref, 0), (far_ref, far_ref.shape[0] // 2), (r2_ref, 0), (r1_ref, 0), own)
        keys_t = jnp.concatenate([ref[base : base + tok, head_cols(j)].T for ref, base in every], axis=1)
        ds_all = jnp.concatenate([far_ds_ref[:, cols], middle_ds_ref[:, cols], ds_scr[:, cols]], axis=0)
        dq_t = dot(keys_t, ds_all, NN) * SCALE
        for h in range(group):
            dq_ref[:, head_cols(j * group + h)] = dq_t[:, h * tok : (h + 1) * tok].T.astype(jnp.bfloat16)
        return carry

    lax.fori_loop(0, kv_heads, one_kv_head, 0, unroll=True)


def call(kernel, name, args, out_shape, scratch, keys, products, sizes):
    tok, group, kv_heads, _ = sizes
    whole = pl.BlockSpec(memory_space=pltpu.VMEM)
    pairs = keys * tok * group * kv_heads
    return pl.pallas_call(
        functools.partial(kernel, *sizes),
        in_specs=[whole] * len(args),
        out_specs=tuple(whole for _ in out_shape),
        out_shape=tuple(jax.ShapeDtypeStruct(s, d) for s, d in out_shape),
        scratch_shapes=[pltpu.VMEM(s, d) for s, d in scratch],
        compiler_params=pltpu.CompilerParams(vmem_limit_bytes=40 * 2**20),
        cost_estimate=pl.CostEstimate(
            flops=2 * products * pairs * HEAD_DIM, bytes_accessed=sum(a.size * a.dtype.itemsize for a in args), transcendentals=pairs
        ),
        name=name,
    )(*args)


def per_device(query, key, value, attn_out, out_grad, segments):
    tok = query.shape[0]
    heads = query.shape[1] // HEAD_DIM // CHUNKS
    width = key.shape[1] // CHUNKS
    kv_heads = width // HEAD_DIM
    group = heads // kv_heads
    f32, bf16 = jnp.float32, jnp.bfloat16
    documents = jnp.tile((segments + 1).astype(bf16)[None, :], (16, width // tok))
    stat = ((heads, tok), f32)
    near, far = 3 * tok, 2 * tok
    parts = range(CHUNKS)
    sizes = [(tok, group, kv_heads, c * heads) for c in parts]
    cols = [slice(c * width, (c + 1) * width) for c in parts]
    if FULL1:
        whole_own = jnp.concatenate([key, value, jnp.tile(documents, (1, CHUNKS))], axis=0)
        whole_r2 = shift(whole_own, 2)
        whole_r1 = shift(whole_own, 1)
        own, r2, r1 = ([a[:, cols[c]] for c in parts] for a in (whole_own, whole_r2, whole_r1))
    else:
        own = [jnp.concatenate([key[:, cols[c]], value[:, cols[c]], documents], axis=0) for c in parts]
        r2 = [shift(own[c], 2) for c in parts]
        r1 = [shift(own[c], 1) for c in parts]
    near_out, r43 = [], []
    for c in parts:
        relayed = jnp.concatenate([r2[c], r1[c]], axis=0)
        if near_out and EARLY:
            relayed, _ = lax.optimization_barrier((relayed, near_out[-1]))
        r43.append(shift(relayed, 2))
        near_out.append(call(
            near_stats_kernel, "near_stats", (query, out_grad, attn_out, own[c], r1[c], r2[c]),
            (stat, stat) + (stat,) * (CHUNKS if c == 0 else 0), (((near, tok), f32),), near, 1, sizes[c],
        ))
    pending = ((2 * tok, width), bf16)
    saved = ((far, heads * tok), bf16)
    far_out, x43 = [], []
    for c in parts:
        near_top, near_sum = near_out[c][:2]
        delta = near_out[0][2 + c]
        far_out.append(call(
            far_kernel, "far_gradients", (query, out_grad, own[c], r43[c], near_top, near_sum, delta),
            (((4 * tok, width), bf16), stat, saved),
            (((far, tok), f32), ((far, group * tok), bf16)), far, 4, sizes[c],
        ))
        x43.append(shift(far_out[c][0], -2))
    sums, middle_ds = [], []
    for c in parts:
        lse = far_out[c][1]
        if sums and not FULL2:
            lse, _ = lax.optimization_barrier((lse, sums[-1]))
        d2, d1, ds = call(
            middle_kernel, "near_middle", (query, out_grad, own[c], r1[c], r2[c], lse, near_out[0][2 + c]),
            (pending, pending, saved), (((far, tok), f32), ((far, group * tok), bf16)), far, 4, sizes[c],
        )
        middle_ds.append(ds)
        sums.append((
            (d2.astype(f32) + x43[c][: 2 * tok].astype(f32)).astype(bf16),
            (d1.astype(f32) + x43[c][2 * tok :].astype(f32)).astype(bf16),
        ))
    if FULL2:
        sums = [tuple(jnp.concatenate(a, axis=1) for a in zip(*sums))]
        sums = lax.optimization_barrier(sums)
    back = [(shift(sum2, -2), shift(sum1, -1)) for sum2, sum1 in sums]
    dq, mine = [], []
    for c in parts:
        lse, _ = lax.optimization_barrier((far_out[c][1], sums[-1]))
        query_grad, terms = call(
            own_kernel, "near_own",
            (query, out_grad, own[c], r1[c], r2[c], r43[c], lse, near_out[0][2 + c], far_out[c][2], middle_ds[c]),
            (((tok, heads * HEAD_DIM), bf16), ((2 * tok, width), f32)),
            (((tok, tok), f32), ((tok, group * tok), bf16), ((tok, heads * tok), bf16)), tok, 9, sizes[c],
        )
        dq.append(query_grad)
        mine.append(terms)
    if FULL2:
        mine = [jnp.concatenate(mine, axis=1)]
    total = [(m + y2.astype(f32) + y1.astype(f32)).astype(bf16) for m, (y2, y1) in zip(mine, back)]
    total = lax.optimization_barrier(jnp.concatenate(total, axis=1))
    return jnp.concatenate(dq, axis=1), total[:tok], total[tok:]


def solution(mesh):
    split = P(AXES, None)
    return jax.shard_map(
        per_device,
        mesh=mesh,
        in_specs=(split, split, split, split, split, P(AXES)),
        out_specs=(split, split, split),
        check_vma=False,
    )
```
